512 devices in a mesh: aux: 128 (over z, y, core), occ: 4 (over x).
Axes of the slice: x: 4, y: 4, z: 16, core: 2. Of those that a mesh axis runs over, the one named last changes fastest.
Arguments:
- orbital_slab: bfloat16 [4, 6144, 3072], P('occ', 'aux'), may hold values from -0.65625 to 0.65625
- eps_occ: float32 [4], replicated, may hold values from -1.5 to -0.3
- eps_vir: float32 [3072], replicated, may hold values from 0.069 to 8.5
Outputs:
- gamma: float32 [4, 6144, 3072], P('occ', 'aux')
- pair_energy: float32 [4, 3072], P('occ')
The draws below stay inside these ranges and needn't reach their ends.
All inputs are finite; a program needn't handle non-finite values.
Results may differ from the reference program's by a relative error of at most 0.0033.
Values may be sent and summed in bfloat16 or wider, within the bound.
A program may use at most 64 MiB of HBM per device.

```python
import jax
import jax.numpy as jnp
from jax import lax

NV = 3072
NAUX = 6144
B_BLOCKS = 8
NOCC_W = 4


def draw_eps_vir(key, part):
    key = jax.random.fold_in(key, 11)
    ramp = 0.1 + 5.9 * jnp.arange(NV, dtype=jnp.float32) / NV
    factor = jax.random.uniform(key, (NV,), jnp.float32, 0.7, 1.4)
    return (ramp * factor).astype(jnp.float32)


def block_scale(key, dims, cuts, smallest, top_value):
    factor_of = 1.0
    for position, parts in cuts:
        draws = jax.random.uniform(jax.random.fold_in(jax.random.fold_in(key, 6), position), (parts,), jnp.float32, smallest / len(cuts), top_value / len(cuts))
        factor_of = factor_of * jnp.repeat(jnp.exp(draws), dims[position] // parts).reshape((-1,) + (1,) * (len(dims) - 1 - position))
    return factor_of


def bell_draw(own_key, shape, deviation, reach, pieces=(), kind=jnp.bfloat16):
    values = deviation * jax.random.normal(own_key, shape, jnp.float32)
    if pieces:
        values = values * block_scale(own_key, shape, pieces, -0.22, 0.18)
    return jnp.clip(values, -reach, reach).astype(kind)


def setup_inputs(seed: int = 0) -> dict:
    seeds = jax.random.split(jax.random.key(seed), 4)
    orbital_slab = bell_draw(seeds[0], (NOCC_W, NAUX, NV), 0.11, 0.65625, ((0, 4), (1, 128)))
    eps_occ = jnp.clip(jax.random.uniform(seeds[1], (NOCC_W,), jnp.float32, -1.5, -0.3), -1.5, -0.3)
    eps_vir = draw_eps_vir(jax.random.fold_in(seeds[3], 71), 0)
    return {"orbital_slab": orbital_slab, "eps_occ": eps_occ, "eps_vir": eps_vir}


def reference(orbital_slab, eps_occ, eps_vir):
    partner_slab = orbital_slab[0]
    col_width = NV // B_BLOCKS
    gammas = []
    energies = []
    for orbital in range(NOCC_W):
        own_orbital = orbital_slab[orbital]
        pair_ints = jnp.dot(own_orbital.T, partner_slab, preferred_element_type=jnp.float32)
        denominator = eps_occ[orbital] + eps_occ[0] - eps_vir[:, None] - eps_vir[None, :]
        amplitude = pair_ints / denominator
        amp_low = amplitude.astype(jnp.bfloat16)
        energies.append(jnp.sum(pair_ints * amplitude, axis=1) / NV)
        accumulated = jnp.zeros((NAUX, NV), jnp.float32)
        for block_index in range(B_BLOCKS):
            start = block_index * col_width
            part = jnp.dot(partner_slab[:, start:start + col_width], amp_low[:, start:start + col_width].T,
                           preferred_element_type=jnp.float32).astype(jnp.bfloat16)
            part = lax.optimization_barrier(part)
            accumulated = accumulated + part.astype(jnp.float32)
        gammas.append(accumulated)
    return jnp.stack(gammas), jnp.stack(energies)
```

```python
import functools

import jax
import jax.numpy as jnp
from jax import lax
from jax.experimental import pallas as pl
from jax.experimental.pallas import tpu as pltpu
from jax.sharding import PartitionSpec as P

MESH = pl.DeviceIdType.MESH
CHUNKS = 3
LANES = 128


def al(value, step):
    return pl.multiple_of(value, step)


def kernel(cfg, slab, eocc, evir, gamma, energy,
           lbuf, rsrc, rbuf, cpart, cx, csum, ax, asum, bx, amp, gpart, psend, px, fin, gb,
           etile, esum, ex, eall,
           lsend, lrecv, lps, lpr, scs, scr, rzs, rzr, xs, xr, ys, yr, ps, pr, gs, gr, es, er, ezs, ezr, eps_s, eps_r, loc):
    nz, rows, nv = cfg
    hz = nz // 2
    group = CHUNKS * LANES
    half = nv // 2
    quart = half // 4
    aux = lax.axis_index("aux")
    x = lax.axis_index("occ")
    z, y, c = aux // 8, (aux // 2) % 4, aux % 2
    s, m = z % 2, z // 2
    own_r = hz - 1 + s
    base = hz * s
    swap = ((y + 1) // 2) % 2
    hi = jnp.where(c == 0, swap, y // 2)
    lo = jnp.where(c == 0, y // 2, swap)
    slot = 4 * c + 2 * hi + lo
    y_a = jnp.where(c == 0, y + 1 - 2 * (y % 2), 3 - y)
    y_b = jnp.where(c == 0, 3 - y, y + 1 - 2 * (y % 2))

    def dev(zz=None, yy=None, cc=None, xx=None):
        zz = z if zz is None else zz
        yy = y if yy is None else yy
        cc = c if cc is None else cc
        xx = x if xx is None else xx
        return (zz * 8 + yy * 2 + cc, xx)

    def copy(src, dst, ssem, rsem, device):
        return pltpu.make_async_remote_copy(
            src_ref=src, dst_ref=dst, send_sem=ssem, recv_sem=rsem, device_id=device, device_id_type=MESH)

    def zmod(v):
        return (v + 2 * nz) % nz

    def rot(zs, mt):
        return (zs - 2 * mt + hz - 1 + 2 * nz) % nz

    dev_a, dev_b, dev_c, dev_p = dev(yy=y_a), dev(yy=y_b), dev(cc=1 - c), dev(zz=z + 1 - 2 * s)
    right, left = (x + 1) % 4, (x + 3) % 4

    def toward(d):
        return zmod(z + d * (1 - 2 * ((d + s) % 2)))

    def behind(d):
        return zmod(z - d * (1 - 2 * s))

    def rrow(r):
        return pl.ds(al(r * rows, 16), rows)

    def cols(start, width):
        return pl.ds(al(start, LANES), width)

    bar = pltpu.get_barrier_semaphore()
    zs_seen = []
    partners = [dev_a, dev_b, dev_c, dev(xx=right), dev(xx=left), dev(xx=(x + 2) % 4)]
    back = list(range(1, hz))
    ahead = [d for d in sorted({1, 2} | set(range(2, hz, 2)))]
    for d in back:
        partners.append(dev(zz=behind(d)))
    for d in ahead:
        if nz - d not in back and d not in zs_seen:
            partners.append(dev(zz=zmod(z + d * (1 - 2 * s))))
    for p in partners:
        pl.semaphore_signal(bar, inc=1, device_id=p, device_id_type=MESH)
    pl.semaphore_wait(bar, len(partners))

    def l_send(j, d):
        zt = toward(d)
        mt = zt // 2
        return copy(slab.at[0, :, cols(mt * group + j * LANES, LANES)], lbuf.at[j, rrow(rot(z, mt)), :],
                    lsend.at[j, d - 1], lrecv.at[j, d - 1], dev(zz=zt))

    def l_wait(j, d):
        r = rot(behind(d), m)
        copy(lbuf.at[j, rrow(r), :], lbuf.at[j, rrow(r), :], lsend.at[j, d - 1], lrecv.at[j, d - 1], dev_p).wait_recv()

    def l_relay(j, at):
        part = pl.ds(al(at * rows, 16), hz * rows)
        return copy(lbuf.at[j, part, :], lbuf.at[j, part, :], lps.at[j], lpr.at[j], dev_p)

    def l_start(j):
        for d in range(1, hz):
            l_send(j, d).start()

    def l_pass(j):
        for d in range(1, hz):
            l_wait(j, d)
        l_relay(j, base).start()

    def scatter(p, xt):
        return copy(slab.at[0, :, cols(p * half + xt * quart, quart)], rsrc.at[p], scs.at[p, xt - 1], scr.at[p],
                    dev(xx=xt))

    @pl.when(x == 0)
    def _():
        for p in range(2):
            for xt in (2, 1, 3):
                scatter(p, xt).start()

    etile[...] = jnp.zeros_like(etile)
    locals_ = []
    for j in range(CHUNKS):
        locals_.append(pltpu.make_async_copy(
            slab.at[0, :, cols(m * group + j * LANES, LANES)], lbuf.at[j, rrow(own_r), :], loc.at[j]))
    for l in locals_:
        l.start()
    l_start(0)

    @pl.when(x == 0)
    def _():
        for p in range(2):
            cp = pltpu.make_async_copy(slab.at[0, :, cols(p * half, quart)], rsrc.at[p], loc.at[CHUNKS + p])
            cp.start()
            cp.wait()

    @pl.when(x != 0)
    def _():
        for p in range(2):
            copy(rsrc.at[p], rsrc.at[p], scs.at[p, 0], scr.at[p], dev_p).wait_recv()

    own_q = cols(x * quart, quart)
    reach = (hz, hz - 1)

    def source(direction, d):
        return zmod(z - d) if direction == 0 else zmod(z + d)

    def rz_copy(direction, d):
        step = 1 if d == 1 else 2
        zt = zmod(z + step) if direction == 0 else zmod(z - step)
        if d == 1:
            zsrc, src = z, rsrc.at[1 - s]
        elif d == 2:
            zsrc, src = z, rsrc.at[s]
        else:
            zsrc = source(direction, d - 2)
            src = rbuf.at[rrow(rot(zsrc, m)), own_q]
        return copy(src, rbuf.at[rrow(rot(zsrc, zt // 2)), own_q], rzs.at[direction, d - 1], rzr.at[direction, d - 1],
                    dev(zz=zt))

    def rz_wait(direction, d):
        here = rbuf.at[rrow(rot(source(direction, d), m)), own_q]
        copy(here, here, rzs.at[direction, d - 1], rzr.at[direction, d - 1], dev_p).wait_recv()

    items = [(0, 0)]
    for k in range(1, hz // 2 + 1):
        for d in (2 * k - 1, 2 * k):
            for direction in range(2):
                if d <= reach[direction]:
                    items.append((direction, d))

    def item_row(item):
        direction, d = item
        return rrow(own_r) if d == 0 else rrow(rot(source(direction, d), m))

    def x_send(item, side):
        t = items.index(item)
        dst = rbuf.at[item_row(item), own_q]
        src = rsrc.at[s] if item[1] == 0 else dst
        return copy(src, dst, xs.at[side, t], xr.at[side, t], dev(xx=right if side == 0 else left))

    def x_wait(item, side):
        t = items.index(item)
        q = (left, right, (x + 2) % 4)[side]
        here = rbuf.at[item_row(item), cols(q * quart, quart)]
        copy(here, here, xs.at[side, t], xr.at[side, t], dev_p).wait_recv()

    def x_forward(item):
        t = items.index(item)
        if t % 2 == 0:
            q, to = left, right
        else:
            q, to = right, left
        here = rbuf.at[item_row(item), cols(q * quart, quart)]
        return copy(here, here, xs.at[2, t], xr.at[2, t], dev(xx=to))

    def x_pass(done):
        for item in done:
            x_wait(item, 0)
            x_wait(item, 1)
            x_forward(item).start()

    sent_z = [(direction, d) for d in (1, 2) for direction in range(2) if d <= reach[direction]]
    for direction, d in sent_z:
        rz_copy(direction, d).start()
    own_copy = pltpu.make_async_copy(rsrc.at[s], rbuf.at[rrow(own_r), own_q], loc.at[CHUNKS])
    own_copy.start()
    for side in range(2):
        x_send((0, 0), side).start()
    for l in locals_:
        l.wait()
    own_copy.wait()
    previous = [(0, 0)]
    for k in range(1, hz // 2 + 1):
        now = [i for i in items if i[1] in (2 * k - 1, 2 * k)]
        for item in now:
            direction, d = item
            rz_wait(direction, d)
            if d + 2 <= reach[direction]:
                rz_copy(direction, d + 2).start()
                sent_z.append((direction, d + 2))
            for side in range(2):
                x_send(item, side).start()
        if k == 1:
            l_pass(0)
            l_start(1)
        if k == 2:
            l_pass(1)
            l_start(2)
        x_pass(previous)
        previous = now
    if hz // 2 < 2:
        l_pass(1)
        l_start(2)
    l_pass(2)
    x_pass(previous)
    for item in items:
        x_wait(item, 2)

    lane = lax.broadcasted_iota(jnp.int32, (16, LANES), 1)
    sub = lax.broadcasted_iota(jnp.int32, (16, LANES), 0)
    mask = lane == sub + 16 * slot

    def y_copy(j, step):
        if step == 0:
            src, dst, to = cpart.at[j, pl.ds(al((1 - c) * 64, 64), 64), :], cx.at[j], dev_c
        elif step == 1:
            src, dst, to = csum.at[j, pl.ds(al((1 - hi) * 32, 32), 32), :], ax.at[j], dev_a
        elif step == 2:
            src, dst, to = asum.at[j, pl.ds(al((1 - lo) * 16, 16), 16), :], bx.at[j], dev_b
        elif step == 3:
            src, to = amp.at[j, pl.ds(al(16 * slot, 16), 16), :], dev_b
            dst = src
        elif step == 4:
            src, to = amp.at[j, pl.ds(al(64 * c + 32 * hi, 32), 32), :], dev_a
            dst = src
        else:
            src, to = amp.at[j, pl.ds(al(64 * c, 64), 64), :], dev_c
            dst = src
        return copy(src, dst, ys.at[j, step], yr.at[j, step], to)

    def y_wait(j, step):
        if step < 3:
            y_copy(j, step).wait_recv()
            return
        if step == 3:
            here = amp.at[j, pl.ds(al(64 * c + 32 * hi + 16 * (1 - lo), 16), 16), :]
        elif step == 4:
            here = amp.at[j, pl.ds(al(64 * c + 32 * (1 - hi), 32), 32), :]
        else:
            here = amp.at[j, pl.ds(al(64 * (1 - c), 64), 64), :]
        copy(here, here, ys.at[j, step], yr.at[j, step], dev_p).wait_recv()

    tile = half // 3

    def stage0(j):
        other = hz * (1 - s)
        l_relay(j, other).wait_recv()

        @pl.loop(0, 3)
        def _(t):
            at = cols(t * tile, tile)
            cpart[j, :, at] = lax.dot_general(lbuf[j], rbuf[:, at], (((0,), (0,)), ((), ())),
                                              preferred_element_type=jnp.float32)
        y_copy(j, 0).start()

    def stage1(j):
        y_wait(j, 0)
        csum[j] = cpart[j, pl.ds(al(c * 64, 64), 64), :] + cx[j]
        y_copy(j, 1).start()

    def stage2(j):
        y_wait(j, 1)
        asum[j] = csum[j, pl.ds(al(hi * 32, 32), 32), :] + ax[j]
        y_copy(j, 2).start()

    def stage3(j):
        y_wait(j, 2)
        ints = asum[j, pl.ds(al(lo * 16, 16), 16), :] + bx[j]
        first_row = jnp.broadcast_to(evir[0:1, cols(m * group + j * LANES, LANES)], (16, LANES))
        first = jnp.sum(jnp.where(mask, first_row, 0.0), axis=1, keepdims=True)
        second = evir[0:1, cols(s * half, half)]
        denominator = (eocc[x] + eocc[0]) - first - second
        amplitude = ints / denominator
        amp[j, pl.ds(al(16 * slot, 16), 16), :] = amplitude.astype(jnp.bfloat16)
        y_copy(j, 3).start()
        e = jnp.sum(ints * amplitude, axis=1, keepdims=True)
        etile[j:j + 1, :] = jnp.sum(jnp.where(mask, e, 0.0), axis=0, keepdims=True)

    def stage4(j):
        y_wait(j, 3)
        y_copy(j, 4).start()

    def stage5(j):
        y_wait(j, 4)
        y_copy(j, 5).start()

    span = hz * rows

    def p_copy(j):
        return copy(psend.at[j], px.at[j], ps.at[j], pr.at[j], dev_p)

    def stage6(j):
        y_wait(j, 5)

        def part(at):
            return lax.dot_general(rbuf[pl.ds(al(at * rows, 16), span), :], amp[j], (((1,), (1,)), ((), ())),
                                   preferred_element_type=jnp.float32)
        psend[j] = part(hz * (1 - s)).astype(jnp.bfloat16)
        p_copy(j).start()
        gpart[j] = part(base)

    def g_copy(j, d):
        block = jnp.where(s == 0, hz - 1 - d, d)
        return copy(fin.at[j, rrow(block), :], gb.at[j, d - 1], gs.at[j, d - 1], gr.at[j, d - 1], dev(zz=behind(d)))

    def stage7(j):
        p_copy(j).wait_recv()
        total = gpart[j] + px[j].astype(jnp.float32)
        gpart[j] = total
        fin[j] = total.astype(jnp.bfloat16)
        for d in range(hz - 1, 0, -1):
            g_copy(j, d).start()
        mine = jnp.where(s == 0, hz - 1, 0)
        gamma[0, :, cols(m * group + j * LANES, LANES)] = gpart[j, rrow(mine), :]

    def stage8(j):
        for d in range(1, hz):
            g_copy(j, d).wait_recv()
            gamma[0, :, cols((toward(d) // 2) * group + j * LANES, LANES)] = gb[j, d - 1].astype(jnp.float32)

    stages = (stage0, stage1, stage2, stage3, stage4, stage5, stage6, stage7, stage8)

    def e_copy(step):
        src = (etile, esum.at[0], esum.at[1])[step]
        return copy(src, ex.at[step], es.at[step], er.at[step], (dev_b, dev_a, dev_c)[step])

    def ez_copy(d):
        zt = toward(d)
        return copy(eall.at[own_r], eall.at[rot(z, zt // 2)], ezs.at[d - 1], ezr.at[d - 1], dev(zz=zt))

    def ep_copy(at):
        here = eall.at[pl.ds(at, hz)]
        return copy(here, here, eps_s.at[0], eps_r.at[0], dev_p)

    def e_stage(n):
        if n == 3:
            e_copy(0).start()
        elif n == 4:
            e_copy(0).wait_recv()
            esum[0] = etile[...] + ex[0]
            e_copy(1).start()
        elif n == 5:
            e_copy(1).wait_recv()
            esum[1] = esum[0] + ex[1]
            e_copy(2).start()
        elif n == 6:
            e_copy(2).wait_recv()
            eall[own_r] = esum[1] + ex[2]
            for d in range(1, hz):
                ez_copy(d).start()
        elif n == 7:
            for d in range(1, hz):
                here = eall.at[rot(behind(d), m)]
                copy(here, here, ezs.at[d - 1], ezr.at[d - 1], dev_p).wait_recv()
            ep_copy(base).start()
        elif n == 8:
            ep_copy(hz * (1 - s)).wait_recv()
            for mm in range(hz):
                both = eall[rot(2 * mm, m)] + eall[rot(2 * mm + 1, m)]
                for j in range(CHUNKS):
                    energy[0:1, mm * group + j * LANES: mm * group + (j + 1) * LANES] = both[j:j + 1, :] / nv

    for tick in range(len(stages) + CHUNKS - 1):
        for j in range(CHUNKS):
            n = tick - j
            if 0 <= n < len(stages):
                stages[n](j)
                if j == CHUNKS - 1:
                    e_stage(n)

    @pl.when(x == 0)
    def _():
        for p in range(2):
            for xt in (2, 1, 3):
                scatter(p, xt).wait_send()

    for j in range(CHUNKS):
        for d in range(1, hz):
            l_send(j, d).wait_send()
            g_copy(j, d).wait_send()
        l_relay(j, base).wait_send()
        for step in range(6):
            y_copy(j, step).wait_send()
        p_copy(j).wait_send()
    for direction, d in sent_z:
        rz_copy(direction, d).wait_send()
    for item in items:
        for side in range(2):
            x_send(item, side).wait_send()
        x_forward(item).wait_send()
    for step in range(3):
        e_copy(step).wait_send()
    for d in range(1, hz):
        ez_copy(d).wait_send()
    ep_copy(base).wait_send()


def body(nz, orbital_slab, eps_occ, eps_vir):
    _, rows, nv = orbital_slab.shape
    hz = nz // 2
    half, quart = nv // 2, nv // 8
    span = hz * rows
    f32, bf16 = jnp.float32, jnp.bfloat16
    dma = pltpu.SemaphoreType.DMA
    items = nz
    scratch = [
        pltpu.VMEM((CHUNKS, nz * rows, LANES), bf16),
        pltpu.VMEM((2, rows, quart), bf16),
        pltpu.VMEM((nz * rows, half), bf16),
        pltpu.VMEM((CHUNKS, 128, half), f32),
        pltpu.VMEM((CHUNKS, 64, half), f32),
        pltpu.VMEM((CHUNKS, 64, half), f32),
        pltpu.VMEM((CHUNKS, 32, half), f32),
        pltpu.VMEM((CHUNKS, 32, half), f32),
        pltpu.VMEM((CHUNKS, 16, half), f32),
        pltpu.VMEM((CHUNKS, 128, half), bf16),
        pltpu.VMEM((CHUNKS, span, LANES), f32),
        pltpu.VMEM((CHUNKS, span, LANES), bf16),
        pltpu.VMEM((CHUNKS, span, LANES), bf16),
        pltpu.VMEM((CHUNKS, span, LANES), bf16),
        pltpu.VMEM((CHUNKS, hz - 1, rows, LANES), bf16),
        pltpu.VMEM((8, LANES), f32),
        pltpu.VMEM((2, 8, LANES), f32),
        pltpu.VMEM((3, 8, LANES), f32),
        pltpu.VMEM((nz, 8, LANES), f32),
        dma((CHUNKS, hz - 1)), dma((CHUNKS, hz - 1)), dma((CHUNKS,)), dma((CHUNKS,)),
        dma((2, 3)), dma((2,)),
        dma((2, hz)), dma((2, hz)),
        dma((3, items)), dma((3, items)),
        dma((CHUNKS, 6)), dma((CHUNKS, 6)),
        dma((CHUNKS,)), dma((CHUNKS,)),
        dma((CHUNKS, hz - 1)), dma((CHUNKS, hz - 1)),
        dma((3,)), dma((3,)),
        dma((hz - 1,)), dma((hz - 1,)),
        dma((1,)), dma((1,)),
        dma((CHUNKS + 2,)),
    ]
    vmem = pl.BlockSpec(memory_space=pltpu.VMEM)
    return pl.pallas_call(
        functools.partial(kernel, (nz, rows, nv)),
        out_shape=(jax.ShapeDtypeStruct((1, rows, nv), f32), jax.ShapeDtypeStruct((1, nv), f32)),
        in_specs=[vmem, pl.BlockSpec(memory_space=pltpu.SMEM), vmem],
        out_specs=(vmem, vmem),
        scratch_shapes=scratch,
        compiler_params=pltpu.CompilerParams(
            collective_id=0, has_side_effects=True, vmem_limit_bytes=48 * 1024 * 1024),
        cost_estimate=pl.CostEstimate(flops=1812 * 10**6, bytes_accessed=10**6, transcendentals=0),
    )(orbital_slab, eps_occ, eps_vir.reshape(1, nv))


def solution(mesh):
    nz = mesh.shape["aux"] // 8
    return jax.shard_map(
        functools.partial(body, nz),
        mesh=mesh,
        in_specs=(P("occ", "aux", None), P(), P()),
        out_specs=(P("occ", "aux", None), P("occ", None)),
        check_vma=False,
    )
```

```python
import functools

import jax
import jax.numpy as jnp
from jax import lax
from jax.experimental import pallas as pl
from jax.experimental.pallas import tpu as pltpu
from jax.sharding import PartitionSpec as P

MESH = pl.DeviceIdType.MESH
CHUNKS = 3
LANES = 128
ORDER = (
    ("c", 0), ("l", 1), ("s", 0), ("l", 2), ("c", 1), ("s", 1), ("c", 2), ("t", 0),
    ("s", 2), ("g", 0), ("t", 1), ("d", 0), ("g", 1), ("t", 2), ("e", 2), ("d", 1),
    ("g", 2), ("e", 3), ("r", 0), ("d", 2), ("e", 4), ("r", 1), ("r", 2), ("e", 5),
    ("o", 0), ("o", 1), ("e", 6), ("o", 2),
)


def al(value, step):
    return pl.multiple_of(value, step)


def kernel(cfg, slab, eocc, evir_in, gamma, energy,
           evir, lbuf, rsrc, rbuf, cpart, cx, csum, yx, amp, gpart, psend, px, fin, gb,
           etile, esum, ex, eall,
           lsend, lrecv, lps, lpr, scs, scr, rzs, rzr, xs, xr, cs, cr, ys, yr, ds, dr, ps, pr, gs, gr, es, er, ezs, ezr, eps_s, eps_r, loc):
    nz, rows, nv = cfg
    hz = nz // 2
    group = CHUNKS * LANES
    half = nv // 2
    quart = half // 4
    aux = lax.axis_index("aux")
    x = lax.axis_index("occ")
    z, y, c = aux // 8, (aux // 2) % 4, aux % 2
    s, m = z % 2, z // 2
    own_r = hz - 1 + s
    base = hz * s
    slot = 4 * c + y

    def dev(zz=None, yy=None, cc=None, xx=None):
        zz = z if zz is None else zz
        yy = y if yy is None else yy
        cc = c if cc is None else cc
        xx = x if xx is None else xx
        return (zz * 8 + yy * 2 + cc, xx)

    def copy(src, dst, ssem, rsem, device):
        return pltpu.make_async_remote_copy(
            src_ref=src, dst_ref=dst, send_sem=ssem, recv_sem=rsem, device_id=device, device_id_type=MESH)

    def zmod(v):
        return (v + 2 * nz) % nz

    def rot(zs, mt):
        return (zs - 2 * mt + hz - 1 + 2 * nz) % nz

    dev_c, dev_p = dev(cc=1 - c), dev(zz=z + 1 - 2 * s)
    right, left = (x + 1) % 4, (x + 3) % 4

    def toward(d):
        return zmod(z + d * (1 - 2 * ((d + s) % 2)))

    def behind(d):
        return zmod(z - d * (1 - 2 * s))

    def rrow(r):
        return pl.ds(al(r * rows, 16), rows)

    def cols(start, width):
        return pl.ds(al(start, LANES), width)

    evir_copy = pltpu.make_async_copy(evir_in, evir, loc.at[CHUNKS + 2])
    evir_copy.start()

    bar = pltpu.get_barrier_semaphore()
    partners = [dev_c, dev(yy=(y + 1) % 4), dev(yy=(y + 2) % 4), dev(yy=(y + 3) % 4), dev(xx=right), dev(xx=left), dev(xx=(x + 2) % 4)]
    back = list(range(1, hz))
    ahead = [d for d in sorted({1, 2} | set(range(2, hz, 2)))]
    for d in back:
        partners.append(dev(zz=behind(d)))
    for d in ahead:
        if nz - d not in back:
            partners.append(dev(zz=zmod(z + d * (1 - 2 * s))))
    for p in partners:
        pl.semaphore_signal(bar, inc=1, device_id=p, device_id_type=MESH)
    pl.semaphore_wait(bar, len(partners))

    def l_send(j, d):
        zt = toward(d)
        mt = zt // 2
        return copy(slab.at[0, :, cols(mt * group + j * LANES, LANES)], lbuf.at[j, rrow(rot(z, mt)), :],
                    lsend.at[j, d - 1], lrecv.at[j, d - 1], dev(zz=zt))

    def l_wait(j, d):
        r = rot(behind(d), m)
        copy(lbuf.at[j, rrow(r), :], lbuf.at[j, rrow(r), :], lsend.at[j, d - 1], lrecv.at[j, d - 1], dev_p).wait_recv()

    def l_relay(j, at):
        part = pl.ds(al(at * rows, 16), hz * rows)
        return copy(lbuf.at[j, part, :], lbuf.at[j, part, :], lps.at[j], lpr.at[j], dev_p)

    def l_start(j):
        for d in range(1, hz):
            l_send(j, d).start()

    def l_pass(j):
        for d in range(1, hz):
            l_wait(j, d)
        l_relay(j, base).start()

    def scatter(p, xt):
        return copy(slab.at[0, :, cols(p * half + xt * quart, quart)], rsrc.at[p], scs.at[p, xt - 1], scr.at[p],
                    dev(xx=xt))

    @pl.when(x == 0)
    def _():
        for p in range(2):
            for xt in (2, 1, 3):
                scatter(p, xt).start()

    etile[...] = jnp.zeros_like(etile)
    locals_ = []
    for j in range(CHUNKS):
        locals_.append(pltpu.make_async_copy(
            slab.at[0, :, cols(m * group + j * LANES, LANES)], lbuf.at[j, rrow(own_r), :], loc.at[j]))
    for l in locals_:
        l.start()
    l_start(0)

    @pl.when(x == 0)
    def _():
        for p in range(2):
            cp = pltpu.make_async_copy(slab.at[0, :, cols(p * half, quart)], rsrc.at[p], loc.at[CHUNKS + p])
            cp.start()
            cp.wait()

    @pl.when(x != 0)
    def _():
        for p in range(2):
            copy(rsrc.at[p], rsrc.at[p], scs.at[p, 0], scr.at[p], dev_p).wait_recv()

    own_q = cols(x * quart, quart)
    reach = (hz, hz - 1)

    def source(direction, d):
        return zmod(z - d) if direction == 0 else zmod(z + d)

    def rz_copy(direction, d):
        step = 1 if d == 1 else 2
        zt = zmod(z + step) if direction == 0 else zmod(z - step)
        if d == 1:
            zsrc, src = z, rsrc.at[1 - s]
        elif d == 2:
            zsrc, src = z, rsrc.at[s]
        else:
            zsrc = source(direction, d - 2)
            src = rbuf.at[rrow(rot(zsrc, m)), own_q]
        return copy(src, rbuf.at[rrow(rot(zsrc, zt // 2)), own_q], rzs.at[direction, d - 1], rzr.at[direction, d - 1],
                    dev(zz=zt))

    def rz_wait(direction, d):
        here = rbuf.at[rrow(rot(source(direction, d), m)), own_q]
        copy(here, here, rzs.at[direction, d - 1], rzr.at[direction, d - 1], dev_p).wait_recv()

    items = [(0, 0)]
    for k in range(1, hz // 2 + 1):
        for d in (2 * k - 1, 2 * k):
            for direction in range(2):
                if d <= reach[direction]:
                    items.append((direction, d))

    def item_row(item):
        direction, d = item
        return rrow(own_r) if d == 0 else rrow(rot(source(direction, d), m))

    def x_send(item, side):
        t = items.index(item)
        dst = rbuf.at[item_row(item), own_q]
        src = rsrc.at[s] if item[1] == 0 else dst
        return copy(src, dst, xs.at[side, t], xr.at[side, t], dev(xx=right if side == 0 else left))

    def x_wait(item, side):
        t = items.index(item)
        q = (left, right, (x + 2) % 4)[side]
        here = rbuf.at[item_row(item), cols(q * quart, quart)]
        copy(here, here, xs.at[side, t], xr.at[side, t], dev_p).wait_recv()

    def x_forward(item):
        t = items.index(item)
        if t % 2 == 0:
            q, to = left, right
        else:
            q, to = right, left
        here = rbuf.at[item_row(item), cols(q * quart, quart)]
        return copy(here, here, xs.at[2, t], xr.at[2, t], dev(xx=to))

    def x_pass(done):
        for item in done:
            x_wait(item, 0)
            x_wait(item, 1)
            x_forward(item).start()

    sent_z = [(direction, d) for d in (1, 2) for direction in range(2) if d <= reach[direction]]
    for direction, d in sent_z:
        rz_copy(direction, d).start()
    own_copy = pltpu.make_async_copy(rsrc.at[s], rbuf.at[rrow(own_r), own_q], loc.at[CHUNKS])
    own_copy.start()
    for side in range(2):
        x_send((0, 0), side).start()
    for l in locals_:
        l.wait()
    own_copy.wait()
    evir_copy.wait()
    previous = [(0, 0)]
    for k in range(1, hz // 2 + 1):
        now = [i for i in items if i[1] in (2 * k - 1, 2 * k)]
        for item in now:
            direction, d = item
            rz_wait(direction, d)
            if d + 2 <= reach[direction]:
                rz_copy(direction, d + 2).start()
                sent_z.append((direction, d + 2))
            for side in range(2):
                x_send(item, side).start()
        if k == hz // 2:
            for j in range(1, CHUNKS):
                l_start(j)
        x_pass(previous)
        previous = now
        if k == hz // 2 - 1:
            l_pass(0)
    if hz // 2 < 2:
        l_pass(0)
    x_pass(previous)
    for item in items:
        x_wait(item, 2)

    lane = lax.broadcasted_iota(jnp.int32, (16, LANES), 1)
    sub = lax.broadcasted_iota(jnp.int32, (16, LANES), 0)
    mask = lane == sub + 16 * slot

    def y_peer(n):
        return (y + n) % 4

    def c_copy(j):
        return copy(cpart.at[j, pl.ds(al((1 - c) * 64, 64), 64), :], cx.at[j], cs.at[j], cr.at[j], dev_c)

    def y_copy(j, n):
        to = y_peer(n)
        return copy(csum.at[j, pl.ds(al(16 * to, 16), 16), :], yx.at[j, n - 1], ys.at[0, j, n - 1],
                    yr.at[0, j, n - 1], dev(yy=to))

    def a_copy(j, n):
        here = amp.at[j, pl.ds(al(16 * slot, 16), 16), :]
        return copy(here, here, ys.at[1, j, n - 1], yr.at[1, j, n - 1], dev(yy=y_peer(n)))

    def a_wait(j, n):
        here = amp.at[j, pl.ds(al(64 * c + 16 * y_peer(-n), 16), 16), :]
        copy(here, here, ys.at[1, j, n - 1], yr.at[1, j, n - 1], dev_c).wait_recv()

    def d_copy(j, side):
        here = amp.at[j, pl.ds(al(64 * side, 64), 64), :]
        return copy(here, here, ds.at[j], dr.at[j], dev_c)

    tile = half // 3

    def stage0(j):
        other = hz * (1 - s)
        l_relay(j, other).wait_recv()

        @pl.loop(0, 3)
        def _(t):
            at = cols(t * tile, tile)
            cpart[j, :, at] = lax.dot_general(lbuf[j], rbuf[:, at], (((0,), (0,)), ((), ())),
                                              preferred_element_type=jnp.float32)
        c_copy(j).start()

    def stage1(j):
        c_copy(j).wait_recv()
        csum[j] = cpart[j, pl.ds(al(c * 64, 64), 64), :] + cx[j]
        for n in (2, 1, 3):
            y_copy(j, n).start()

    def stage2(j):
        for n in (1, 3, 2):
            y_copy(j, n).wait_recv()
        ints = (csum[j, pl.ds(al(16 * y, 16), 16), :] + yx[j, 0]) + (yx[j, 1] + yx[j, 2])
        first_row = jnp.broadcast_to(evir[0:1, cols(m * group + j * LANES, LANES)], (16, LANES))
        first = jnp.sum(jnp.where(mask, first_row, 0.0), axis=1, keepdims=True)
        second = evir[0:1, cols(s * half, half)]
        denominator = (eocc[x] + eocc[0]) - first - second
        amplitude = ints / denominator
        amp[j, pl.ds(al(16 * slot, 16), 16), :] = amplitude.astype(jnp.bfloat16)
        for n in (2, 1, 3):
            a_copy(j, n).start()
        e = jnp.sum(ints * amplitude, axis=1, keepdims=True)
        etile[j:j + 1, :] = jnp.sum(jnp.where(mask, e, 0.0), axis=0, keepdims=True)

    def stage3(j):
        for n in (1, 3, 2):
            a_wait(j, n)
        d_copy(j, c).start()

    span = hz * rows

    def p_copy(j):
        return copy(psend.at[j], px.at[j], ps.at[j], pr.at[j], dev_p)

    def stage4(j):
        d_copy(j, 1 - c).wait_recv()

        def part(at):
            return lax.dot_general(rbuf[pl.ds(al(at * rows, 16), span), :], amp[j], (((1,), (1,)), ((), ())),
                                   preferred_element_type=jnp.float32)
        psend[j] = part(hz * (1 - s)).astype(jnp.bfloat16)
        p_copy(j).start()
        gpart[j] = part(base)

    def g_copy(j, d):
        block = jnp.where(s == 0, hz - 1 - d, d)
        return copy(fin.at[j, rrow(block), :], gb.at[j, d - 1], gs.at[j, d - 1], gr.at[j, d - 1], dev(zz=behind(d)))

    def stage5(j):
        p_copy(j).wait_recv()
        total = gpart[j] + px[j].astype(jnp.float32)
        gpart[j] = total
        fin[j] = total.astype(jnp.bfloat16)
        for d in range(hz - 1, 0, -1):
            g_copy(j, d).start()
        mine = jnp.where(s == 0, hz - 1, 0)
        gamma[0, :, cols(m * group + j * LANES, LANES)] = gpart[j, rrow(mine), :]

    def stage6(j):
        for d in range(1, hz):
            g_copy(j, d).wait_recv()
            gamma[0, :, cols((toward(d) // 2) * group + j * LANES, LANES)] = gb[j, d - 1].astype(jnp.float32)


    def e_copy(n):
        return copy(etile, ex.at[n - 1], es.at[n - 1], er.at[n - 1], dev(yy=y_peer(n)))

    def ec_copy():
        return copy(esum, ex.at[3], es.at[3], er.at[3], dev_c)

    def ez_copy(d):
        zt = toward(d)
        return copy(eall.at[own_r], eall.at[rot(z, zt // 2)], ezs.at[d - 1], ezr.at[d - 1], dev(zz=zt))

    def ep_copy(at):
        here = eall.at[pl.ds(at, hz)]
        return copy(here, here, eps_s.at[0], eps_r.at[0], dev_p)

    def e_stage(n):
        if n == 2:
            for peer in (2, 1, 3):
                e_copy(peer).start()
        elif n == 3:
            for peer in (1, 3, 2):
                e_copy(peer).wait_recv()
            esum[...] = (etile[...] + ex[0]) + (ex[1] + ex[2])
            ec_copy().start()
        elif n == 4:
            ec_copy().wait_recv()
            eall[own_r] = esum[...] + ex[3]
            for d in range(1, hz):
                ez_copy(d).start()
        elif n == 5:
            for d in range(1, hz):
                here = eall.at[rot(behind(d), m)]
                copy(here, here, ezs.at[d - 1], ezr.at[d - 1], dev_p).wait_recv()
            ep_copy(base).start()
        elif n == 6:
            ep_copy(hz * (1 - s)).wait_recv()
            for mm in range(hz):
                both = eall[rot(2 * mm, m)] + eall[rot(2 * mm + 1, m)]
                for j in range(CHUNKS):
                    energy[0:1, mm * group + j * LANES: mm * group + (j + 1) * LANES] = both[j:j + 1, :] / nv

    stages = dict(l=l_pass, c=stage0, s=stage1, t=stage2, g=stage3, d=stage4, r=stage5, o=stage6, e=e_stage)
    for name, n in ORDER:
        stages[name](n)

    @pl.when(x == 0)
    def _():
        for p in range(2):
            for xt in (2, 1, 3):
                scatter(p, xt).wait_send()

    for j in range(CHUNKS):
        for d in range(1, hz):
            l_send(j, d).wait_send()
            g_copy(j, d).wait_send()
        l_relay(j, base).wait_send()
        c_copy(j).wait_send()
        d_copy(j, c).wait_send()
        for n in range(1, 4):
            y_copy(j, n).wait_send()
            a_copy(j, n).wait_send()
        p_copy(j).wait_send()
    for direction, d in sent_z:
        rz_copy(direction, d).wait_send()
    for item in items:
        for side in range(2):
            x_send(item, side).wait_send()
        x_forward(item).wait_send()
    for n in range(1, 4):
        e_copy(n).wait_send()
    ec_copy().wait_send()
    for d in range(1, hz):
        ez_copy(d).wait_send()
    ep_copy(base).wait_send()


def body(nz, orbital_slab, eps_occ, eps_vir):
    _, rows, nv = orbital_slab.shape
    hz = nz // 2
    half, quart = nv // 2, nv // 8
    span = hz * rows
    f32, bf16 = jnp.float32, jnp.bfloat16
    dma = pltpu.SemaphoreType.DMA
    items = nz
    scratch = [
        pltpu.VMEM((1, nv), f32),
        pltpu.VMEM((CHUNKS, nz * rows, LANES), bf16),
        pltpu.VMEM((2, rows, quart), bf16),
        pltpu.VMEM((nz * rows, half), bf16),
        pltpu.VMEM((CHUNKS, 128, half), f32),
        pltpu.VMEM((CHUNKS, 64, half), f32),
        pltpu.VMEM((CHUNKS, 64, half), f32),
        pltpu.VMEM((CHUNKS, 3, 16, half), f32),
        pltpu.VMEM((CHUNKS, 128, half), bf16),
        pltpu.VMEM((CHUNKS, span, LANES), f32),
        pltpu.VMEM((CHUNKS, span, LANES), bf16),
        pltpu.VMEM((CHUNKS, span, LANES), bf16),
        pltpu.VMEM((CHUNKS, span, LANES), bf16),
        pltpu.VMEM((CHUNKS, hz - 1, rows, LANES), bf16),
        pltpu.VMEM((8, LANES), f32),
        pltpu.VMEM((8, LANES), f32),
        pltpu.VMEM((4, 8, LANES), f32),
        pltpu.VMEM((nz, 8, LANES), f32),
        dma((CHUNKS, hz - 1)), dma((CHUNKS, hz - 1)), dma((CHUNKS,)), dma((CHUNKS,)),
        dma((2, 3)), dma((2,)),
        dma((2, hz)), dma((2, hz)),
        dma((3, items)), dma((3, items)),
        dma((CHUNKS,)), dma((CHUNKS,)),
        dma((2, CHUNKS, 3)), dma((2, CHUNKS, 3)),
        dma((CHUNKS,)), dma((CHUNKS,)),
        dma((CHUNKS,)), dma((CHUNKS,)),
        dma((CHUNKS, hz - 1)), dma((CHUNKS, hz - 1)),
        dma((4,)), dma((4,)),
        dma((hz - 1,)), dma((hz - 1,)),
        dma((1,)), dma((1,)),
        dma((CHUNKS + 3,)),
    ]
    vmem = pl.BlockSpec(memory_space=pltpu.VMEM)
    hbm = pl.BlockSpec(memory_space=pl.ANY)
    return pl.pallas_call(
        functools.partial(kernel, (nz, rows, nv)),
        out_shape=(jax.ShapeDtypeStruct((1, rows, nv), f32), jax.ShapeDtypeStruct((1, nv), f32)),
        in_specs=[hbm, pl.BlockSpec(memory_space=pltpu.SMEM), hbm],
        out_specs=(vmem, vmem),
        scratch_shapes=scratch,
        compiler_params=pltpu.CompilerParams(
            collective_id=0, has_side_effects=True, vmem_limit_bytes=56 * 1024 * 1024),
        cost_estimate=pl.CostEstimate(flops=1812 * 10**6, bytes_accessed=10**6, transcendentals=0),
    )(orbital_slab, eps_occ, eps_vir.reshape(1, nv))


def solution(mesh):
    nz = mesh.shape["aux"] // 8
    return jax.shard_map(
        functools.partial(body, nz),
        mesh=mesh,
        in_specs=(P("occ", "aux", None), P(), P()),
        out_specs=(P("occ", "aux", None), P("occ", None)),
        check_vma=False,
    )
```

```python
import functools

import jax
import jax.numpy as jnp
from jax import lax
from jax.experimental import pallas as pl
from jax.experimental.pallas import tpu as pltpu
from jax.sharding import PartitionSpec as P

MESH = pl.DeviceIdType.MESH
CHUNKS = 3
LANES = 128
ORDER = (
    ("l", 1), ("c", 0), ("l", 2), ("s", 0), ("w", 0), ("C", 1), ("c", 1), ("S", 1), ("s", 1), ("C", 2), ("c", 2), ("w", 1),
    ("t", 0), ("S", 2), ("s", 2), ("w", 2), ("g", 0), ("t", 1), ("d", 0), ("g", 1), ("t", 2), ("e", 2), ("d", 1),
    ("g", 2), ("e", 3), ("r", 0), ("d", 2), ("e", 4), ("r", 1), ("w", 3), ("r", 2), ("e", 5),
    ("o", 0), ("w", 4), ("o", 1), ("w", 5), ("e", 6), ("w", 6), ("o", 2),
)
L_AT = (4, 4)
P0_AT = 2
LAG = 1


def al(value, step):
    return pl.multiple_of(value, step)


def kernel(cfg, slab, eocc, evir_in, gamma, energy,
           evir, lbuf, rsrc, rbuf, cpart, cx, csum, yx, amp, gpart, psend, px, fin, gb,
           etile, esum, ex, eall,
           lsend, lrecv, lps, lpr, scs, scr, rzs, rzr, xs, xr, cs, cr, ys, yr, ds, dr, ps, pr, gs, gr, es, er, ezs, ezr, eps_s, eps_r, loc):
    nz, rows, nv = cfg
    hz = nz // 2
    group = CHUNKS * LANES
    half = nv // 2
    quart = half // 4
    aux = lax.axis_index("aux")
    x = lax.axis_index("occ")
    z, y, c = aux // 8, (aux // 2) % 4, aux % 2
    s, m = z % 2, z // 2
    own_r = hz - 1 + s
    base = hz * s
    slot = 4 * c + y

    def dev(zz=None, yy=None, cc=None, xx=None):
        zz = z if zz is None else zz
        yy = y if yy is None else yy
        cc = c if cc is None else cc
        xx = x if xx is None else xx
        return (zz * 8 + yy * 2 + cc, xx)

    def copy(src, dst, ssem, rsem, device):
        return pltpu.make_async_remote_copy(
            src_ref=src, dst_ref=dst, send_sem=ssem, recv_sem=rsem, device_id=device, device_id_type=MESH)

    def zmod(v):
        return (v + 2 * nz) % nz

    def rot(zs, mt):
        return (zs - 2 * mt + hz - 1 + 2 * nz) % nz

    dev_c, dev_p = dev(cc=1 - c), dev(zz=z + 1 - 2 * s)
    right, left = (x + 1) % 4, (x + 3) % 4

    def toward(d):
        return zmod(z + d * (1 - 2 * ((d + s) % 2)))

    def behind(d):
        return zmod(z - d * (1 - 2 * s))

    def rrow(r):
        return pl.ds(al(r * rows, 16), rows)

    def cols(start, width):
        return pl.ds(al(start, LANES), width)

    evir_copy = pltpu.make_async_copy(evir_in, evir, loc.at[CHUNKS + 2])
    evir_copy.start()

    bar = pltpu.get_barrier_semaphore()
    partners = [dev_c, dev(yy=(y + 1) % 4), dev(yy=(y + 2) % 4), dev(yy=(y + 3) % 4), dev(xx=right), dev(xx=left), dev(xx=(x + 2) % 4)]
    back = list(range(1, hz))
    ahead = [d for d in sorted({1, 2} | set(range(2, hz, 2)))]
    for d in back:
        partners.append(dev(zz=behind(d)))
    for d in ahead:
        if nz - d not in back:
            partners.append(dev(zz=zmod(z + d * (1 - 2 * s))))
    for p in partners:
        pl.semaphore_signal(bar, inc=1, device_id=p, device_id_type=MESH)
    pl.semaphore_wait(bar, len(partners))

    def l_send(j, d):
        zt = toward(d)
        mt = zt // 2
        return copy(slab.at[0, :, cols(mt * group + j * LANES, LANES)], lbuf.at[j, rrow(rot(z, mt)), :],
                    lsend.at[j, d - 1], lrecv.at[j, d - 1], dev(zz=zt))

    def l_wait(j, d):
        r = rot(behind(d), m)
        copy(lbuf.at[j, rrow(r), :], lbuf.at[j, rrow(r), :], lsend.at[j, d - 1], lrecv.at[j, d - 1], dev_p).wait_recv()

    def l_relay(j, at):
        part = pl.ds(al(at * rows, 16), hz * rows)
        return copy(lbuf.at[j, part, :], lbuf.at[j, part, :], lps.at[j], lpr.at[j], dev_p)

    def l_start(j):
        for d in range(1, hz):
            l_send(j, d).start()

    def l_pass(j):
        for d in range(1, hz):
            l_wait(j, d)
        l_relay(j, base).start()

    def scatter(p, xt):
        return copy(slab.at[0, :, cols(p * half + xt * quart, quart)], rsrc.at[p], scs.at[p, xt - 1], scr.at[p],
                    dev(xx=xt))

    @pl.when(x == 0)
    def _():
        for p in range(2):
            for xt in (2, 1, 3):
                scatter(p, xt).start()

    etile[...] = jnp.zeros_like(etile)
    locals_ = []
    for j in range(CHUNKS):
        locals_.append(pltpu.make_async_copy(
            slab.at[0, :, cols(m * group + j * LANES, LANES)], lbuf.at[j, rrow(own_r), :], loc.at[j]))
    for l in locals_:
        l.start()
    l_start(0)

    @pl.when(x == 0)
    def _():
        for p in range(2):
            cp = pltpu.make_async_copy(slab.at[0, :, cols(p * half, quart)], rsrc.at[p], loc.at[CHUNKS + p])
            cp.start()
            cp.wait()

    @pl.when(x != 0)
    def _():
        for p in range(2):
            copy(rsrc.at[p], rsrc.at[p], scs.at[p, 0], scr.at[p], dev_p).wait_recv()

    def rel(n):
        return slice(n * quart, (n + 1) * quart)

    own_q = rel(0)
    reach = (hz, hz - 1)

    def source(direction, d):
        return zmod(z - d) if direction == 0 else zmod(z + d)

    def rz_copy(direction, d):
        step = 1 if d == 1 else 2
        zt = zmod(z + step) if direction == 0 else zmod(z - step)
        if d == 1:
            zsrc, src = z, rsrc.at[1 - s]
        elif d == 2:
            zsrc, src = z, rsrc.at[s]
        else:
            zsrc = source(direction, d - 2)
            src = rbuf.at[rrow(rot(zsrc, m)), own_q]
        return copy(src, rbuf.at[rrow(rot(zsrc, zt // 2)), own_q], rzs.at[direction, d - 1], rzr.at[direction, d - 1],
                    dev(zz=zt))

    def rz_wait(direction, d):
        here = rbuf.at[rrow(rot(source(direction, d), m)), own_q]
        copy(here, here, rzs.at[direction, d - 1], rzr.at[direction, d - 1], dev_p).wait_recv()

    items = [(0, 0)]
    for k in range(1, hz // 2 + 1):
        for d in (2 * k - 1, 2 * k):
            for direction in range(2):
                if d <= reach[direction]:
                    items.append((direction, d))

    def item_row(item):
        direction, d = item
        return rrow(own_r) if d == 0 else rrow(rot(source(direction, d), m))

    def x_send(item, side):
        t = items.index(item)
        row = item_row(item)
        src = rsrc.at[s] if item[1] == 0 else rbuf.at[row, own_q]
        return copy(src, rbuf.at[row, rel((3, 1)[side])], xs.at[side, t], xr.at[side, t],
                    dev(xx=right if side == 0 else left))

    def x_wait(item, side):
        t = items.index(item)
        here = rbuf.at[item_row(item), rel((3, 1, 2)[side])]
        copy(here, here, xs.at[side, t], xr.at[side, t], dev_p).wait_recv()

    def x_forward(item):
        t = items.index(item)
        row = item_row(item)
        n, to = (3, right) if t % 2 == 0 else (1, left)
        return copy(rbuf.at[row, rel(n)], rbuf.at[row, rel(2)], xs.at[2, t], xr.at[2, t], dev(xx=to))

    def x_pass(done):
        for item in done:
            x_wait(item, 0)
            x_wait(item, 1)
            x_forward(item).start()

    sent_z = [(direction, d) for d in (1, 2) for direction in range(2) if d <= reach[direction]]
    for direction, d in sent_z:
        rz_copy(direction, d).start()
    own_copy = pltpu.make_async_copy(rsrc.at[s], rbuf.at[rrow(own_r), own_q], loc.at[CHUNKS])
    own_copy.start()
    for side in range(2):
        x_send((0, 0), side).start()
    for l in locals_:
        l.wait()
    own_copy.wait()
    evir_copy.wait()
    lane = lax.broadcasted_iota(jnp.int32, (16, LANES), 1)
    sub = lax.broadcasted_iota(jnp.int32, (16, LANES), 0)
    mask = lane == sub + 16 * slot

    def y_peer(n):
        return (y + n) % 4

    def piece(part):
        return slice(0, quart) if part == 0 else slice(quart, half)

    def c_copy(j, part):
        return copy(cpart.at[j, pl.ds(al((1 - c) * 64, 64), 64), piece(part)], cx.at[j, :, piece(part)],
                    cs.at[part, j], cr.at[part, j], dev_c)

    def y_copy(j, n, part):
        to = y_peer(n)
        return copy(csum.at[j, pl.ds(al(16 * to, 16), 16), piece(part)], yx.at[j, n - 1, :, piece(part)],
                    ys.at[part, j, n - 1], yr.at[part, j, n - 1], dev(yy=to))

    def a_copy(j, n):
        here = amp.at[j, pl.ds(al(16 * slot, 16), 16), :]
        return copy(here, here, ys.at[2, j, n - 1], yr.at[2, j, n - 1], dev(yy=y_peer(n)))

    def a_wait(j, n):
        here = amp.at[j, pl.ds(al(64 * c + 16 * y_peer(-n), 16), 16), :]
        copy(here, here, ys.at[2, j, n - 1], yr.at[2, j, n - 1], dev_c).wait_recv()

    def d_copy(j, side):
        here = amp.at[j, pl.ds(al(64 * side, 64), 64), :]
        return copy(here, here, ds.at[j], dr.at[j], dev_c)

    def integrals(j, at):
        cpart[j, :, at] = lax.dot_general(lbuf[j], rbuf[:, at], (((0,), (0,)), ((), ())),
                                          preferred_element_type=jnp.float32)

    def stage0a(j):
        l_relay(j, hz * (1 - s)).wait_recv()
        integrals(j, piece(0))
        c_copy(j, 0).start()

    def stage0(j):
        @pl.loop(1, 4)
        def _(n):
            integrals(j, cols(n * quart, quart))
        c_copy(j, 1).start()

    def stage1(j, part):
        c_copy(j, part).wait_recv()
        csum[j, :, piece(part)] = cpart[j, pl.ds(al(c * 64, 64), 64), piece(part)] + cx[j, :, piece(part)]
        for n in (2, 1, 3):
            y_copy(j, n, part).start()

    def stage2(j):
        for part in range(2):
            for n in (1, 3, 2):
                y_copy(j, n, part).wait_recv()
        first_row = jnp.broadcast_to(evir[0:1, cols(m * group + j * LANES, LANES)], (16, LANES))
        first = jnp.sum(jnp.where(mask, first_row, 0.0), axis=1, keepdims=True)
        e = jnp.zeros((16, 1), jnp.float32)
        for q in range(4):
            at = rel(q)
            ints = (csum[j, pl.ds(al(16 * y, 16), 16), at] + yx[j, 0, :, at]) + (yx[j, 1, :, at] + yx[j, 2, :, at])
            second = evir[0:1, cols(s * half + ((x + q) % 4) * quart, quart)]
            denominator = (eocc[x] + eocc[0]) - first - second
            amplitude = ints / denominator
            amp[j, pl.ds(al(16 * slot, 16), 16), at] = amplitude.astype(jnp.bfloat16)
            e = e + jnp.sum(ints * amplitude, axis=1, keepdims=True)
        for n in (2, 1, 3):
            a_copy(j, n).start()
        etile[j:j + 1, :] = jnp.sum(jnp.where(mask, e, 0.0), axis=0, keepdims=True)

    def stage3(j):
        for n in (1, 3, 2):
            a_wait(j, n)
        d_copy(j, c).start()

    span = hz * rows

    def p_copy(j):
        return copy(psend.at[j], px.at[j], ps.at[j], pr.at[j], dev_p)

    def stage4(j):
        d_copy(j, 1 - c).wait_recv()

        def part(at):
            return lax.dot_general(rbuf[pl.ds(al(at * rows, 16), span), :], amp[j], (((1,), (1,)), ((), ())),
                                   preferred_element_type=jnp.float32)
        psend[j] = part(hz * (1 - s)).astype(jnp.bfloat16)
        p_copy(j).start()
        gpart[j] = part(base)

    def g_copy(j, d):
        block = jnp.where(s == 0, hz - 1 - d, d)
        return copy(fin.at[j, rrow(block), :], gb.at[j, d - 1], gs.at[j, d - 1], gr.at[j, d - 1], dev(zz=behind(d)))

    def stage5(j):
        p_copy(j).wait_recv()
        total = gpart[j] + px[j].astype(jnp.float32)
        gpart[j] = total
        fin[j] = total.astype(jnp.bfloat16)
        for d in range(hz - 1, 0, -1):
            g_copy(j, d).start()
        mine = jnp.where(s == 0, hz - 1, 0)
        gamma[0, :, cols(m * group + j * LANES, LANES)] = gpart[j, rrow(mine), :]

    def stage6(j):
        for d in range(1, hz):
            g_copy(j, d).wait_recv()
            gamma[0, :, cols((toward(d) // 2) * group + j * LANES, LANES)] = gb[j, d - 1].astype(jnp.float32)


    def e_copy(n):
        return copy(etile, ex.at[n - 1], es.at[n - 1], er.at[n - 1], dev(yy=y_peer(n)))

    def ec_copy():
        return copy(esum, ex.at[3], es.at[3], er.at[3], dev_c)

    def ez_copy(d):
        zt = toward(d)
        return copy(eall.at[own_r], eall.at[rot(z, zt // 2)], ezs.at[d - 1], ezr.at[d - 1], dev(zz=zt))

    def ep_copy(at):
        here = eall.at[pl.ds(at, hz)]
        return copy(here, here, eps_s.at[0], eps_r.at[0], dev_p)

    def e_stage(n):
        if n == 2:
            for peer in (2, 1, 3):
                e_copy(peer).start()
        elif n == 3:
            for peer in (1, 3, 2):
                e_copy(peer).wait_recv()
            esum[...] = (etile[...] + ex[0]) + (ex[1] + ex[2])
            ec_copy().start()
        elif n == 4:
            ec_copy().wait_recv()
            eall[own_r] = esum[...] + ex[3]
            for d in range(1, hz):
                ez_copy(d).start()
        elif n == 5:
            for d in range(1, hz):
                here = eall.at[rot(behind(d), m)]
                copy(here, here, ezs.at[d - 1], ezr.at[d - 1], dev_p).wait_recv()
            ep_copy(base).start()
        elif n == 6:
            ep_copy(hz * (1 - s)).wait_recv()
            for mm in range(hz):
                both = eall[rot(2 * mm, m)] + eall[rot(2 * mm + 1, m)]
                for j in range(CHUNKS):
                    energy[0:1, mm * group + j * LANES: mm * group + (j + 1) * LANES] = both[j:j + 1, :] / nv

    def drain(n):
        if n == 0:
            @pl.when(x == 0)
            def _():
                for p in range(2):
                    for xt in (2, 1, 3):
                        scatter(p, xt).wait_send()
            for direction, d in sent_z:
                rz_copy(direction, d).wait_send()
        elif n == 1:
            for item in items:
                for side in range(2):
                    x_send(item, side).wait_send()
                x_forward(item).wait_send()
        elif n == 2:
            for j in range(CHUNKS):
                for d in range(1, hz):
                    l_send(j, d).wait_send()
                l_relay(j, base).wait_send()
        elif n == 3:
            for j in range(CHUNKS):
                d_copy(j, c).wait_send()
                for part in range(2):
                    c_copy(j, part).wait_send()
                    for n in range(1, 4):
                        y_copy(j, n, part).wait_send()
                for n in range(1, 4):
                    a_copy(j, n).wait_send()
            for n in range(1, 4):
                e_copy(n).wait_send()
            ec_copy().wait_send()
        else:
            j = n - 4
            p_copy(j).wait_send()
            for d in range(1, hz):
                g_copy(j, d).wait_send()
            if j == CHUNKS - 1:
                for d in range(1, hz):
                    ez_copy(d).wait_send()
                ep_copy(base).wait_send()

    stages = dict(l=l_pass, C=stage0a, c=stage0, S=lambda j: stage1(j, 0), s=lambda j: stage1(j, 1), t=stage2, g=stage3,
                  d=stage4, r=stage5, o=stage6, e=e_stage, w=drain)

    pending = [[(0, 0)]]
    for k in range(1, hz // 2 + 1):
        now = [i for i in items if i[1] in (2 * k - 1, 2 * k)]
        for item in now:
            direction, d = item
            rz_wait(direction, d)
            if d + 2 <= reach[direction]:
                rz_copy(direction, d + 2).start()
                sent_z.append((direction, d + 2))
            for side in range(2):
                x_send(item, side).start()
        for j in range(1, CHUNKS):
            if k == min(L_AT[j - 1], hz // 2):
                l_start(j)
        pending.append(now)
        if len(pending) > LAG:
            x_pass(pending.pop(0))
        if k == min(P0_AT, hz // 2 - 1):
            l_pass(0)
    if hz // 2 < 2:
        l_pass(0)
    stages["C"](0)
    for done in pending:
        x_pass(done)
    stages["S"](0)
    for item in items:
        x_wait(item, 2)

    for name, n in ORDER:
        stages[name](n)


def body(nz, orbital_slab, eps_occ, eps_vir):
    _, rows, nv = orbital_slab.shape
    hz = nz // 2
    half, quart = nv // 2, nv // 8
    span = hz * rows
    f32, bf16 = jnp.float32, jnp.bfloat16
    dma = pltpu.SemaphoreType.DMA
    items = nz
    scratch = [
        pltpu.VMEM((1, nv), f32),
        pltpu.VMEM((CHUNKS, nz * rows, LANES), bf16),
        pltpu.VMEM((2, rows, quart), bf16),
        pltpu.VMEM((nz * rows, half), bf16),
        pltpu.VMEM((CHUNKS, 128, half), f32),
        pltpu.VMEM((CHUNKS, 64, half), f32),
        pltpu.VMEM((CHUNKS, 64, half), f32),
        pltpu.VMEM((CHUNKS, 3, 16, half), f32),
        pltpu.VMEM((CHUNKS, 128, half), bf16),
        pltpu.VMEM((CHUNKS, span, LANES), f32),
        pltpu.VMEM((CHUNKS, span, LANES), bf16),
        pltpu.VMEM((CHUNKS, span, LANES), bf16),
        pltpu.VMEM((CHUNKS, span, LANES), bf16),
        pltpu.VMEM((CHUNKS, hz - 1, rows, LANES), bf16),
        pltpu.VMEM((8, LANES), f32),
        pltpu.VMEM((8, LANES), f32),
        pltpu.VMEM((4, 8, LANES), f32),
        pltpu.VMEM((nz, 8, LANES), f32),
        dma((CHUNKS, hz - 1)), dma((CHUNKS, hz - 1)), dma((CHUNKS,)), dma((CHUNKS,)),
        dma((2, 3)), dma((2,)),
        dma((2, hz)), dma((2, hz)),
        dma((3, items)), dma((3, items)),
        dma((2, CHUNKS)), dma((2, CHUNKS)),
        dma((3, CHUNKS, 3)), dma((3, CHUNKS, 3)),
        dma((CHUNKS,)), dma((CHUNKS,)),
        dma((CHUNKS,)), dma((CHUNKS,)),
        dma((CHUNKS, hz - 1)), dma((CHUNKS, hz - 1)),
        dma((4,)), dma((4,)),
        dma((hz - 1,)), dma((hz - 1,)),
        dma((1,)), dma((1,)),
        dma((CHUNKS + 3,)),
    ]
    vmem = pl.BlockSpec(memory_space=pltpu.VMEM)
    hbm = pl.BlockSpec(memory_space=pl.ANY)
    return pl.pallas_call(
        functools.partial(kernel, (nz, rows, nv)),
        out_shape=(jax.ShapeDtypeStruct((1, rows, nv), f32), jax.ShapeDtypeStruct((1, nv), f32)),
        in_specs=[hbm, pl.BlockSpec(memory_space=pltpu.SMEM), hbm],
        out_specs=(vmem, vmem),
        scratch_shapes=scratch,
        compiler_params=pltpu.CompilerParams(
            collective_id=0, has_side_effects=True, vmem_limit_bytes=56 * 1024 * 1024),
        cost_estimate=pl.CostEstimate(flops=1812 * 10**6, bytes_accessed=10**6, transcendentals=0),
    )(orbital_slab, eps_occ, eps_vir.reshape(1, nv))


def solution(mesh):
    nz = mesh.shape["aux"] // 8
    return jax.shard_map(
        functools.partial(body, nz),
        mesh=mesh,
        in_specs=(P("occ", "aux", None), P(), P()),
        out_specs=(P("occ", "aux", None), P("occ", None)),
        check_vma=False,
    )
```

```python
import functools

import jax
import jax.numpy as jnp
from jax import lax
from jax.experimental import pallas as pl
from jax.experimental.pallas import tpu as pltpu
from jax.sharding import PartitionSpec as P

MESH = pl.DeviceIdType.MESH
CHUNKS = 3
LANES = 128
ORDER = (
    ("l", 1), ("c", 0), ("l", 2), ("s", 0), ("w", 0), ("C", 1), ("c", 1), ("S", 1), ("s", 1), ("C", 2), ("c", 2), ("w", 1),
    ("t", 0), ("S", 2), ("s", 2), ("w", 2), ("g", 0), ("t", 1), ("d", 0), ("g", 1), ("t", 2), ("e", 2), ("d", 1),
    ("g", 2), ("e", 3), ("r", 0), ("d", 2), ("e", 4), ("r", 1), ("w", 3), ("r", 2), ("e", 5),
    ("o", 0), ("w", 4), ("o", 1), ("w", 5), ("e", 6), ("w", 6), ("o", 2),
)
L_AT = (4, 4)
P0_AT = 2
LAG = 1


def al(value, step):
    return pl.multiple_of(value, step)


def kernel(cfg, slab, eocc, evir_in, gamma, energy,
           evir, lbuf, rsrc, rbuf, cpart, cx, csum, yx, amp, gpart, psend, px, fin, gb,
           etile, esum, ex, eall,
           lsend, lrecv, lps, lpr, scs, scr, rzs, rzr, xs, xr, cs, cr, ys, yr, ds, dr, ps, pr, gs, gr, es, er, ezs, ezr, eps_s, eps_r, loc):
    nz, rows, nv = cfg
    hz = nz // 2
    group = CHUNKS * LANES
    half = nv // 2
    quart = half // 4
    aux = lax.axis_index("aux")
    x = lax.axis_index("occ")
    z, y, c = aux // 8, (aux // 2) % 4, aux % 2
    s, m = z % 2, z // 2
    own_r = hz - 1 + s
    base = hz * s
    slot = 4 * c + y

    def dev(zz=None, yy=None, cc=None, xx=None):
        zz = z if zz is None else zz
        yy = y if yy is None else yy
        cc = c if cc is None else cc
        xx = x if xx is None else xx
        return (zz * 8 + yy * 2 + cc, xx)

    def copy(src, dst, ssem, rsem, device):
        return pltpu.make_async_remote_copy(
            src_ref=src, dst_ref=dst, send_sem=ssem, recv_sem=rsem, device_id=device, device_id_type=MESH)

    def zmod(v):
        return (v + 2 * nz) % nz

    def rot(zs, mt):
        return (zs - 2 * mt + hz - 1 + 2 * nz) % nz

    dev_c, dev_p = dev(cc=1 - c), dev(zz=z + 1 - 2 * s)
    right, left = (x + 1) % 4, (x + 3) % 4

    def toward(d):
        return zmod(z + d * (1 - 2 * ((d + s) % 2)))

    def behind(d):
        return zmod(z - d * (1 - 2 * s))

    def rrow(r):
        return pl.ds(al(r * rows, 16), rows)

    def cols(start, width):
        return pl.ds(al(start, LANES), width)

    evir_copy = pltpu.make_async_copy(evir_in, evir, loc.at[CHUNKS + 2])
    evir_copy.start()

    bar = pltpu.get_barrier_semaphore()
    partners = [dev_c, dev(yy=(y + 1) % 4), dev(yy=(y + 2) % 4), dev(yy=(y + 3) % 4), dev(xx=right), dev(xx=left), dev(xx=(x + 2) % 4)]
    back = list(range(1, hz))
    ahead = [d for d in sorted({1, 2} | set(range(2, hz, 2)))]
    for d in back:
        partners.append(dev(zz=behind(d)))
    for d in ahead:
        if nz - d not in back:
            partners.append(dev(zz=zmod(z + d * (1 - 2 * s))))
    for p in partners:
        pl.semaphore_signal(bar, inc=1, device_id=p, device_id_type=MESH)
    pl.semaphore_wait(bar, len(partners))

    def l_send(j, d):
        zt = toward(d)
        mt = zt // 2
        return copy(slab.at[0, :, cols(mt * group + j * LANES, LANES)], lbuf.at[j, rrow(rot(z, mt)), :],
                    lsend.at[j, d - 1], lrecv.at[j, d - 1], dev(zz=zt))

    def l_wait(j, d):
        r = rot(behind(d), m)
        copy(lbuf.at[j, rrow(r), :], lbuf.at[j, rrow(r), :], lsend.at[j, d - 1], lrecv.at[j, d - 1], dev_p).wait_recv()

    def l_relay(j, at):
        part = pl.ds(al(at * rows, 16), hz * rows)
        return copy(lbuf.at[j, part, :], lbuf.at[j, part, :], lps.at[j], lpr.at[j], dev_p)

    def l_start(j):
        for d in range(1, hz):
            l_send(j, d).start()

    def l_pass(j):
        for d in range(1, hz):
            l_wait(j, d)
        l_relay(j, base).start()

    def scatter(p, xt):
        return copy(slab.at[0, :, cols(p * half + xt * quart, quart)], rsrc.at[p], scs.at[p, xt - 1], scr.at[p],
                    dev(xx=xt))

    @pl.when(x == 0)
    def _():
        for p in range(2):
            for xt in (2, 1, 3):
                scatter(p, xt).start()

    etile[...] = jnp.zeros_like(etile)
    locals_ = []
    for j in range(CHUNKS):
        locals_.append(pltpu.make_async_copy(
            slab.at[0, :, cols(m * group + j * LANES, LANES)], lbuf.at[j, rrow(own_r), :], loc.at[j]))
    for l in locals_:
        l.start()
    l_start(0)

    @pl.when(x == 0)
    def _():
        for p in range(2):
            cp = pltpu.make_async_copy(slab.at[0, :, cols(p * half, quart)], rsrc.at[p], loc.at[CHUNKS + p])
            cp.start()
            cp.wait()

    @pl.when(x != 0)
    def _():
        for p in range(2):
            copy(rsrc.at[p], rsrc.at[p], scs.at[p, 0], scr.at[p], dev_p).wait_recv()

    def rel(n):
        return slice(n * quart, (n + 1) * quart)

    own_q = rel(0)
    reach = (hz, hz - 1)

    def source(direction, d):
        return zmod(z - d) if direction == 0 else zmod(z + d)

    def rz_copy(direction, d):
        step = 1 if d == 1 else 2
        zt = zmod(z + step) if direction == 0 else zmod(z - step)
        if d == 1:
            zsrc, src = z, rsrc.at[1 - s]
        elif d == 2:
            zsrc, src = z, rsrc.at[s]
        else:
            zsrc = source(direction, d - 2)
            src = rbuf.at[rrow(rot(zsrc, m)), own_q]
        return copy(src, rbuf.at[rrow(rot(zsrc, zt // 2)), own_q], rzs.at[direction, d - 1], rzr.at[direction, d - 1],
                    dev(zz=zt))

    def rz_wait(direction, d):
        here = rbuf.at[rrow(rot(source(direction, d), m)), own_q]
        copy(here, here, rzs.at[direction, d - 1], rzr.at[direction, d - 1], dev_p).wait_recv()

    items = [(0, 0)]
    for k in range(1, hz // 2 + 1):
        for d in (2 * k - 1, 2 * k):
            for direction in range(2):
                if d <= reach[direction]:
                    items.append((direction, d))

    def item_row(item):
        direction, d = item
        return rrow(own_r) if d == 0 else rrow(rot(source(direction, d), m))

    def x_send(item, side):
        t = items.index(item)
        row = item_row(item)
        src = rsrc.at[s] if item[1] == 0 else rbuf.at[row, own_q]
        return copy(src, rbuf.at[row, rel((3, 1)[side])], xs.at[side, t], xr.at[side, t],
                    dev(xx=right if side == 0 else left))

    def x_wait(item, side):
        t = items.index(item)
        here = rbuf.at[item_row(item), rel((3, 1, 2)[side])]
        copy(here, here, xs.at[side, t], xr.at[side, t], dev_p).wait_recv()

    def x_forward(item):
        t = items.index(item)
        row = item_row(item)
        n, to = (3, right) if t % 2 == 0 else (1, left)
        return copy(rbuf.at[row, rel(n)], rbuf.at[row, rel(2)], xs.at[2, t], xr.at[2, t], dev(xx=to))

    def x_pass(done):
        for item in done:
            x_wait(item, 0)
            x_wait(item, 1)
            x_forward(item).start()

    sent_z = [(direction, d) for d in (1, 2) for direction in range(2) if d <= reach[direction]]
    for direction, d in sent_z:
        rz_copy(direction, d).start()
    own_copy = pltpu.make_async_copy(rsrc.at[s], rbuf.at[rrow(own_r), own_q], loc.at[CHUNKS])
    own_copy.start()
    for side in range(2):
        x_send((0, 0), side).start()
    for l in locals_:
        l.wait()
    own_copy.wait()
    evir_copy.wait()
    lane = lax.broadcasted_iota(jnp.int32, (16, LANES), 1)
    sub = lax.broadcasted_iota(jnp.int32, (16, LANES), 0)
    mask = lane == sub + 16 * slot

    def y_peer(n):
        return (y + n) % 4

    def piece(part):
        return slice(0, quart) if part == 0 else slice(quart, half)

    def c_copy(j, part):
        return copy(cpart.at[j, pl.ds(al((1 - c) * 64, 64), 64), piece(part)], cx.at[j, :, piece(part)],
                    cs.at[part, j], cr.at[part, j], dev_c)

    def y_copy(j, n, part):
        to = y_peer(n)
        return copy(csum.at[j, pl.ds(al(16 * to, 16), 16), piece(part)], yx.at[j, n - 1, :, piece(part)],
                    ys.at[part, j, n - 1], yr.at[part, j, n - 1], dev(yy=to))

    def a_copy(j, n):
        here = amp.at[j, pl.ds(al(16 * slot, 16), 16), :]
        return copy(here, here, ys.at[2, j, n - 1], yr.at[2, j, n - 1], dev(yy=y_peer(n)))

    def a_wait(j, n):
        here = amp.at[j, pl.ds(al(64 * c + 16 * y_peer(-n), 16), 16), :]
        copy(here, here, ys.at[2, j, n - 1], yr.at[2, j, n - 1], dev_c).wait_recv()

    def d_copy(j, side):
        here = amp.at[j, pl.ds(al(64 * side, 64), 64), :]
        return copy(here, here, ds.at[j], dr.at[j], dev_c)

    def integrals(j, at):
        cpart[j, :, at] = lax.dot_general(lbuf[j], rbuf[:, at], (((0,), (0,)), ((), ())),
                                          preferred_element_type=jnp.float32)

    def stage0a(j):
        l_relay(j, hz * (1 - s)).wait_recv()
        integrals(j, piece(0))
        c_copy(j, 0).start()

    def stage0(j):
        @pl.loop(1, 4)
        def _(n):
            integrals(j, cols(n * quart, quart))
        c_copy(j, 1).start()

    def stage1(j, part):
        c_copy(j, part).wait_recv()
        csum[j, :, piece(part)] = cpart[j, pl.ds(al(c * 64, 64), 64), piece(part)] + cx[j, :, piece(part)]
        for n in (2, 1, 3):
            y_copy(j, n, part).start()

    def stage2(j):
        for part in range(2):
            for n in (1, 3, 2):
                y_copy(j, n, part).wait_recv()
        first_row = jnp.broadcast_to(evir[0:1, cols(m * group + j * LANES, LANES)], (16, LANES))
        first = jnp.sum(jnp.where(mask, first_row, 0.0), axis=1, keepdims=True)
        e = jnp.zeros((16, 1), jnp.float32)
        for q in range(4):
            at = rel(q)
            ints = (csum[j, pl.ds(al(16 * y, 16), 16), at] + yx[j, 0, :, at]) + (yx[j, 1, :, at] + yx[j, 2, :, at])
            second = evir[0:1, cols(s * half + ((x + q) % 4) * quart, quart)]
            denominator = (eocc[x] + eocc[0]) - first - second
            amplitude = ints / denominator
            amp[j, pl.ds(al(16 * slot, 16), 16), at] = amplitude.astype(jnp.bfloat16)
            e = e + jnp.sum(ints * amplitude, axis=1, keepdims=True)
        for n in (2, 1, 3):
            a_copy(j, n).start()
        etile[j:j + 1, :] = jnp.sum(jnp.where(mask, e, 0.0), axis=0, keepdims=True)

    def stage3(j):
        for n in (1, 3, 2):
            a_wait(j, n)
        d_copy(j, c).start()

    span = hz * rows

    def p_copy(j, n):
        part = pl.ds(n * (span // 2), span // 2)
        return copy(psend.at[j, part, :], px.at[j, part, :], ps.at[n, j], pr.at[n, j], dev_p)

    def stage4(j):
        d_copy(j, 1 - c).wait_recv()

        def part(at):
            return lax.dot_general(rbuf[pl.ds(al(at * rows, 16), span), :], amp[j], (((1,), (1,)), ((), ())),
                                   preferred_element_type=jnp.float32)
        psend[j] = part(hz * (1 - s)).astype(jnp.bfloat16)
        for n in range(2):
            p_copy(j, n).start()
        gpart[j] = part(base)

    def g_copy(j, d):
        block = jnp.where(s == 0, hz - 1 - d, d)
        return copy(fin.at[j, rrow(block), :], gb.at[j, d - 1], gs.at[j, d - 1], gr.at[j, d - 1], dev(zz=behind(d)))

    def stage5(j):
        for n in range(2):
            p_copy(j, n).wait_recv()
        total = gpart[j] + px[j].astype(jnp.float32)
        gpart[j] = total
        fin[j] = total.astype(jnp.bfloat16)
        for d in range(hz - 1, 0, -1):
            g_copy(j, d).start()
        mine = jnp.where(s == 0, hz - 1, 0)
        gamma[0, :, cols(m * group + j * LANES, LANES)] = gpart[j, rrow(mine), :]

    def stage6(j):
        for d in range(1, hz):
            g_copy(j, d).wait_recv()
            gamma[0, :, cols((toward(d) // 2) * group + j * LANES, LANES)] = gb[j, d - 1].astype(jnp.float32)


    def e_copy(n):
        return copy(etile, ex.at[n - 1], es.at[n - 1], er.at[n - 1], dev(yy=y_peer(n)))

    def ec_copy():
        return copy(esum, ex.at[3], es.at[3], er.at[3], dev_c)

    def ez_copy(d):
        zt = toward(d)
        return copy(eall.at[own_r], eall.at[rot(z, zt // 2)], ezs.at[d - 1], ezr.at[d - 1], dev(zz=zt))

    def ep_copy(at):
        here = eall.at[pl.ds(at, hz)]
        return copy(here, here, eps_s.at[0], eps_r.at[0], dev_p)

    def e_stage(n):
        if n == 2:
            for peer in (2, 1, 3):
                e_copy(peer).start()
        elif n == 3:
            for peer in (1, 3, 2):
                e_copy(peer).wait_recv()
            esum[...] = (etile[...] + ex[0]) + (ex[1] + ex[2])
            ec_copy().start()
        elif n == 4:
            ec_copy().wait_recv()
            eall[own_r] = esum[...] + ex[3]
            for d in range(1, hz):
                ez_copy(d).start()
        elif n == 5:
            for d in range(1, hz):
                here = eall.at[rot(behind(d), m)]
                copy(here, here, ezs.at[d - 1], ezr.at[d - 1], dev_p).wait_recv()
            ep_copy(base).start()
        elif n == 6:
            ep_copy(hz * (1 - s)).wait_recv()
            for mm in range(hz):
                both = eall[rot(2 * mm, m)] + eall[rot(2 * mm + 1, m)]
                for j in range(CHUNKS):
                    energy[0:1, mm * group + j * LANES: mm * group + (j + 1) * LANES] = both[j:j + 1, :] / nv

    def drain(n):
        if n == 0:
            @pl.when(x == 0)
            def _():
                for p in range(2):
                    for xt in (2, 1, 3):
                        scatter(p, xt).wait_send()
            for direction, d in sent_z:
                rz_copy(direction, d).wait_send()
        elif n == 1:
            for item in items:
                for side in range(2):
                    x_send(item, side).wait_send()
                x_forward(item).wait_send()
        elif n == 2:
            for j in range(CHUNKS):
                for d in range(1, hz):
                    l_send(j, d).wait_send()
                l_relay(j, base).wait_send()
        elif n == 3:
            for j in range(CHUNKS):
                d_copy(j, c).wait_send()
                for part in range(2):
                    c_copy(j, part).wait_send()
                    for n in range(1, 4):
                        y_copy(j, n, part).wait_send()
                for n in range(1, 4):
                    a_copy(j, n).wait_send()
            for n in range(1, 4):
                e_copy(n).wait_send()
            ec_copy().wait_send()
        else:
            j = n - 4
            for n in range(2):
                p_copy(j, n).wait_send()
            for d in range(1, hz):
                g_copy(j, d).wait_send()
            if j == CHUNKS - 1:
                for d in range(1, hz):
                    ez_copy(d).wait_send()
                ep_copy(base).wait_send()

    stages = dict(l=l_pass, C=stage0a, c=stage0, S=lambda j: stage1(j, 0), s=lambda j: stage1(j, 1), t=stage2, g=stage3,
                  d=stage4, r=stage5, o=stage6, e=e_stage, w=drain)

    pending = [[(0, 0)]]
    for k in range(1, hz // 2 + 1):
        now = [i for i in items if i[1] in (2 * k - 1, 2 * k)]
        for item in now:
            direction, d = item
            rz_wait(direction, d)
            if d + 2 <= reach[direction]:
                rz_copy(direction, d + 2).start()
                sent_z.append((direction, d + 2))
            for side in range(2):
                x_send(item, side).start()
        for j in range(1, CHUNKS):
            if k == min(L_AT[j - 1], hz // 2):
                l_start(j)
        pending.append(now)
        if len(pending) > LAG:
            x_pass(pending.pop(0))
        if k == min(P0_AT, hz // 2 - 1):
            l_pass(0)
    if hz // 2 < 2:
        l_pass(0)
    stages["C"](0)
    for done in pending:
        x_pass(done)
    stages["S"](0)
    for item in items:
        x_wait(item, 2)

    for name, n in ORDER:
        stages[name](n)


def body(nz, orbital_slab, eps_occ, eps_vir):
    _, rows, nv = orbital_slab.shape
    hz = nz // 2
    half, quart = nv // 2, nv // 8
    span = hz * rows
    f32, bf16 = jnp.float32, jnp.bfloat16
    dma = pltpu.SemaphoreType.DMA
    items = nz
    scratch = [
        pltpu.VMEM((1, nv), f32),
        pltpu.VMEM((CHUNKS, nz * rows, LANES), bf16),
        pltpu.VMEM((2, rows, quart), bf16),
        pltpu.VMEM((nz * rows, half), bf16),
        pltpu.VMEM((CHUNKS, 128, half), f32),
        pltpu.VMEM((CHUNKS, 64, half), f32),
        pltpu.VMEM((CHUNKS, 64, half), f32),
        pltpu.VMEM((CHUNKS, 3, 16, half), f32),
        pltpu.VMEM((CHUNKS, 128, half), bf16),
        pltpu.VMEM((CHUNKS, span, LANES), f32),
        pltpu.VMEM((CHUNKS, span, LANES), bf16),
        pltpu.VMEM((CHUNKS, span, LANES), bf16),
        pltpu.VMEM((CHUNKS, span, LANES), bf16),
        pltpu.VMEM((CHUNKS, hz - 1, rows, LANES), bf16),
        pltpu.VMEM((8, LANES), f32),
        pltpu.VMEM((8, LANES), f32),
        pltpu.VMEM((4, 8, LANES), f32),
        pltpu.VMEM((nz, 8, LANES), f32),
        dma((CHUNKS, hz - 1)), dma((CHUNKS, hz - 1)), dma((CHUNKS,)), dma((CHUNKS,)),
        dma((2, 3)), dma((2,)),
        dma((2, hz)), dma((2, hz)),
        dma((3, items)), dma((3, items)),
        dma((2, CHUNKS)), dma((2, CHUNKS)),
        dma((3, CHUNKS, 3)), dma((3, CHUNKS, 3)),
        dma((CHUNKS,)), dma((CHUNKS,)),
        dma((2, CHUNKS)), dma((2, CHUNKS)),
        dma((CHUNKS, hz - 1)), dma((CHUNKS, hz - 1)),
        dma((4,)), dma((4,)),
        dma((hz - 1,)), dma((hz - 1,)),
        dma((1,)), dma((1,)),
        dma((CHUNKS + 3,)),
    ]
    vmem = pl.BlockSpec(memory_space=pltpu.VMEM)
    hbm = pl.BlockSpec(memory_space=pl.ANY)
    return pl.pallas_call(
        functools.partial(kernel, (nz, rows, nv)),
        out_shape=(jax.ShapeDtypeStruct((1, rows, nv), f32), jax.ShapeDtypeStruct((1, nv), f32)),
        in_specs=[hbm, pl.BlockSpec(memory_space=pltpu.SMEM), hbm],
        out_specs=(vmem, vmem),
        scratch_shapes=scratch,
        compiler_params=pltpu.CompilerParams(
            collective_id=0, has_side_effects=True, vmem_limit_bytes=56 * 1024 * 1024),
        cost_estimate=pl.CostEstimate(flops=1812 * 10**6, bytes_accessed=10**6, transcendentals=0),
    )(orbital_slab, eps_occ, eps_vir.reshape(1, nv))


def solution(mesh):
    nz = mesh.shape["aux"] // 8
    return jax.shard_map(
        functools.partial(body, nz),
        mesh=mesh,
        in_specs=(P("occ", "aux", None), P(), P()),
        out_specs=(P("occ", "aux", None), P("occ", None)),
        check_vma=False,
    )
```
